256 devices in a mesh: sect: 4 (over x), blk: 64 (over y, z, core).
Axes of the slice: x: 4, y: 4, z: 8, core: 2. Of those that a mesh axis runs over, the one named last changes fastest.
Arguments:
- psi_start: float32 [4, 64, 256, 256], P('sect', 'blk'), may hold values from -6 to 6
- kept_sizes: int32 [4, 64], P('sect', 'blk'), may hold values from 64 to 256, as said below
- left_diag: float32 [4, 64, 3, 256, 256], P('sect', 'blk'), as said below
- left_hop: float32 [4, 64, 3, 256, 256], P('sect', 'blk'), may hold values from -0.375 to 0.375
- left_hop_dn: float32 [4, 64, 3, 256, 256], P('sect', 'blk'), may hold values from -0.375 to 0.375
- right_diag: float32 [4, 64, 3, 256, 256], P('sect', 'blk'), as said below
- right_hop: float32 [4, 64, 3, 256, 256], P('sect', 'blk'), may hold values from -0.375 to 0.375
- right_hop_dn: float32 [4, 64, 3, 256, 256], P('sect', 'blk'), may hold values from -0.375 to 0.375
Outputs:
- state: float32 [4, 64, 256, 256], P('sect', 'blk')
- energy: float32 [4], P('sect')
The draws below stay inside these ranges and needn't reach their ends.
Inputs may be any that keep to these rules, and one draw needn't show every extreme that they name: `kept_sizes`: every section's sectors keep between 64 and 256 states; some sector keeps exactly 256. `left_diag`: each block of the charge-conserving channels is symmetric. `right_diag`: each block of the charge-conserving channels is symmetric.
All inputs are finite; a program needn't handle non-finite values.
Results may differ from the reference program's by a relative error of at most 0.00015.
Values sent between devices are 32-bit elements; how exact they have to be, the bound alone decides.
No kernel may reach another device: no remote copies, remote signals or barrier semaphores. Data moves between devices by JAX's collectives and lax.ppermute only.
A program may use at most 64 MiB of HBM per device.

```python
import jax
import jax.numpy as jnp
from jax import lax

B = 256
WC = 3
ITERS = 2
SECTIONS = 4
SECTORS = 64
UPS = 8


def symmetric_blocks(sample):
    return (sample + jnp.swapaxes(sample, -1, -2)) * 0.5 ** 0.5 * B ** (-0.5)


def draw_left_diag(key, part):
    key = jax.random.fold_in(key, 11)
    extent = (SECTIONS, SECTORS, WC, B, B)
    sample = jax.random.normal(key, extent, jnp.float32)
    return symmetric_blocks(sample)


def draw_right_diag(key, part):
    key = jax.random.fold_in(key, 23)
    extent = (SECTIONS, SECTORS, WC, B, B)
    sample = jax.random.normal(key, extent, jnp.float32)
    return symmetric_blocks(sample)


def draw_kept_sizes(key, part):
    key = jax.random.fold_in(key, 37)
    first_key, second_key = jax.random.split(key)
    sizes_drawn = jax.random.randint(first_key, (SECTIONS, SECTORS), B // 4, B + 1)
    position = jax.random.randint(second_key, (), 0, SECTIONS * SECTORS)
    flat_index = jnp.arange(SECTIONS * SECTORS, dtype=jnp.int32).reshape(SECTIONS, SECTORS)
    return jnp.where(flat_index == position, B, sizes_drawn).astype(jnp.int32)


def levels(own_key, dims, pieces, low, largest):
    gain, own = 1.0, jax.random.fold_in(own_key, 6)
    for dim, blocks in pieces:
        draws = jnp.exp(jax.random.uniform(jax.random.fold_in(own, dim), (blocks,), jnp.float32, low / len(pieces), largest / len(pieces)))
        gain = gain * jnp.repeat(draws, dims[dim] // blocks).reshape([-1 if axis == dim else 1 for axis in range(len(dims))])
    return gain


def scatter_about(own_key, shape, deviation, reach, cuts=(), held_as=jnp.bfloat16):
    entries = deviation * jax.random.normal(own_key, shape, jnp.float32)
    if cuts:
        entries = entries * levels(own_key, shape, cuts, -0.22, 0.18)
    return jnp.clip(entries, -reach, reach).astype(held_as)


def setup_inputs(seed: int = 0) -> dict:
    splits = jax.random.split(jax.random.key(seed), 9)
    psi_start = scatter_about(splits[0], (SECTIONS, SECTORS, B, B), 1.0, 6.0, ((0, 4), (1, 64)), jnp.float32)
    kept_sizes = draw_kept_sizes(jax.random.fold_in(splits[8], 71), 0)
    left_diag = draw_left_diag(jax.random.fold_in(splits[8], 71), 0)
    left_hop = scatter_about(splits[3], (SECTIONS, SECTORS, WC, B, B), B ** -0.5, 0.375, ((0, 4), (1, 64)), jnp.float32)
    left_hop_dn = scatter_about(splits[4], (SECTIONS, SECTORS, WC, B, B), B ** -0.5, 0.375, ((0, 4), (1, 64)), jnp.float32)
    right_diag = draw_right_diag(jax.random.fold_in(splits[8], 71), 0)
    right_hop = scatter_about(splits[6], (SECTIONS, SECTORS, WC, B, B), B ** -0.5, 0.375, ((0, 4), (1, 64)), jnp.float32)
    right_hop_dn = scatter_about(splits[7], (SECTIONS, SECTORS, WC, B, B), B ** -0.5, 0.375, ((0, 4), (1, 64)), jnp.float32)
    return dict(psi_start=psi_start, kept_sizes=kept_sizes, left_diag=left_diag, left_hop=left_hop, left_hop_dn=left_hop_dn, right_diag=right_diag, right_hop=right_hop, right_hop_dn=right_hop_dn)


highest = lax.Precision.HIGHEST

def forward_pair(left_env, state_block, right_env):
    inner_term = jnp.einsum('skwab,skbc->skwac', left_env, state_block, precision=highest)
    return jnp.einsum('skwac,skwdc->skad', inner_term, right_env, precision=highest)

def backward_pair(left_env, state_block, right_env):
    inner_term = jnp.einsum('skwba,skbc->skwac', left_env, state_block, precision=highest)
    return jnp.einsum('skwac,skwcd->skad', inner_term, right_env, precision=highest)

def link_factor():
    sector_index = jnp.arange(SECTORS, dtype=jnp.int32)
    return (sector_index % UPS != 0).astype(jnp.float32)[None, :, None, None]

def shift_up(vector, stride):
    zero_block = jnp.zeros_like(vector[:, :stride])
    return jnp.concatenate([zero_block, vector[:, :-stride]], axis=1)

def shift_down(vector, stride):
    zero_block = jnp.zeros_like(vector[:, :stride])
    return jnp.concatenate([vector[:, stride:], zero_block], axis=1)

def apply_operator(vector, diag_left, hop_left, hopdn_left, diag_right, hop_right, hopdn_right, kept_mask):
    link = link_factor()
    local_term = forward_pair(diag_left, vector, diag_right)
    upward = forward_pair(hop_left, shift_up(vector, 1) * link, hop_right)
    downward = shift_down(backward_pair(hop_left, vector, hop_right) * link, 1)
    upward_dn = forward_pair(hopdn_left, shift_up(vector, UPS), hopdn_right)
    downward_dn = shift_down(backward_pair(hopdn_left, vector, hopdn_right), UPS)
    return kept_mask * (local_term + upward + downward + upward_dn + downward_dn)

def section_sum(values):
    return lax.optimization_barrier(jnp.sum(values, axis=(1, 2, 3)))[:, None, None, None]

def davidson(vector, applied, envs, kept_mask):
    lowest = jnp.zeros((vector.shape[0], 1, 1, 1), jnp.float32)
    for iteration in range(ITERS):
        energy_now = section_sum(vector * applied)
        residual = applied - energy_now * vector
        resid_sq = section_sum(residual * residual)
        resid_norm = jnp.sqrt(resid_sq + 1e-12)
        trial = residual / resid_norm
        trial_image = apply_operator(trial, *envs, kept_mask)
        curvature = section_sum(trial * trial_image)
        half_gap = (energy_now - curvature) / 2
        lowest = (energy_now + curvature) / 2 - jnp.sqrt(half_gap * half_gap + resid_norm * resid_norm)
        second_coef = lowest - energy_now
        length = jnp.sqrt(resid_norm * resid_norm + second_coef * second_coef)
        vector = (resid_norm * vector + second_coef * trial) / length
        applied = (resid_norm * applied + second_coef * trial_image) / length
    return (vector, applied, lowest)

def extend_left(left_env, right_factor, vector, env_scale):
    inner_term = jnp.einsum('skwbc,skcd->skwbd', left_env, right_factor, precision=highest)
    return env_scale * jnp.einsum('skba,skwbd->skwad', vector, inner_term, precision=highest)

def reference(psi_start, kept_sizes, left_diag, left_hop, left_hop_dn, right_diag, right_hop, right_hop_dn):
    row_index = jnp.arange(B, dtype=jnp.int32)
    bound = kept_sizes[:, :, None, None]
    kept_mask = ((row_index[None, None, :, None] < bound) & (row_index[None, None, None, :] < bound)).astype(jnp.float32)
    start = kept_mask * psi_start
    vector = start / jnp.sqrt(section_sum(start * start))
    envs = (left_diag, left_hop, left_hop_dn, right_diag, right_hop, right_hop_dn)
    applied = apply_operator(vector, *envs, kept_mask)
    vector, applied, lowest = davidson(vector, applied, envs, kept_mask)
    env_scale = float(SECTORS * B)
    new_diag = extend_left(left_diag, vector, vector, env_scale)
    new_hop = extend_left(left_hop, shift_up(vector, 1) * link_factor(), vector, env_scale)
    new_hop_dn = extend_left(left_hop_dn, shift_up(vector, UPS), vector, env_scale)
    diag_next = jnp.concatenate([left_diag[:1], new_diag[:-1]], axis=0)
    hop_next = jnp.concatenate([left_hop[:1], new_hop[:-1]], axis=0)
    hopdn_next = jnp.concatenate([left_hop_dn[:1], new_hop_dn[:-1]], axis=0)
    envs = (diag_next, hop_next, hopdn_next, right_diag, right_hop, right_hop_dn)
    applied = apply_operator(vector, *envs, kept_mask)
    vector, applied, lowest = davidson(vector, applied, envs, kept_mask)
    return (vector, lowest[:, 0, 0, 0])
```

```python
import jax
import jax.numpy as jnp
from jax import lax
from jax.sharding import PartitionSpec as P

high = lax.Precision.HIGH
EPS = 1e-12


def chain(count, stride):
    ups = [(k, k + 1) for k in range(count - 1) if (k + 1) % stride != 0]
    downs = [(k, k + stride) for k in range(count - stride)]
    return ups, downs


def flipped(pairs):
    return [(target, source) for source, target in pairs]


def total(values):
    count = lax.axis_size("blk")
    step = 1
    while step < count:
        radix = 4 if step * 4 <= count else 2
        parts = [
            lax.ppermute(values, "blk", [(k, k ^ (step * other)) for k in range(count)])
            for other in range(1, radix)
        ]
        if radix == 4:
            values = (values + parts[0]) + (parts[1] + parts[2])
        else:
            values = values + parts[0]
        step *= radix
    return values


def forward_pair(left_env, state_block, right_env):
    inner_term = jnp.einsum("wab,bc->wac", left_env, state_block, precision=high)
    return jnp.einsum("wac,wdc->ad", inner_term, right_env, precision=high)


def backward_pair(left_env, state_block, right_env):
    inner_term = jnp.einsum("wba,bc->wac", left_env, state_block, precision=high)
    return jnp.einsum("wac,wcd->ad", inner_term, right_env, precision=high)


def dot(a, b):
    return jnp.sum(a * b)


def krylov_step(p, normalise, operator, expectation):
    w1 = operator(p)
    first = total(jnp.stack([dot(p, p), dot(p, w1), dot(w1, w1)]))
    w2 = operator(w1)
    norm_sq = first[0] if normalise else jnp.ones((), jnp.float32)
    vv = first[0] / norm_sq
    e = first[1] / norm_sq
    hh = first[2] / norm_sq
    rho = jnp.sqrt(jnp.maximum(hh - e * e, 1e-7 * hh))
    rho = jnp.where(rho > 0, rho, 1.0)
    unit = 1.0 / jnp.sqrt(norm_sq)
    b0 = p * unit
    b1 = (w1 - e * p) * (unit / rho)
    b2 = (w2 - e * w1) * (unit / rho / rho) - (e / rho) * b1
    last = total(jnp.stack([dot(b1, b1), dot(b1, b2), dot(b2, b2), expectation(b2)]))
    h = [
        vv,
        e * (1.0 - vv) / rho,
        last[0],
        last[1],
        last[2],
        (last[3] - e * last[2]) / rho,
    ]
    eps = EPS / rho / rho
    shift = e / rho
    rn = jnp.sqrt(h[2] + eps)
    c = h[3] / (rn * rn) - shift * (eps / (rn * rn))
    low = c / 2 - jnp.sqrt((c / 2) * (c / 2) + rn * rn)
    g = jnp.sqrt(rn * rn + low * low)
    a0 = rn / g
    a1 = low / (g * rn)
    vv1 = a0 * a0 * h[0] + 2 * a0 * a1 * h[1] + a1 * a1 * h[2]
    e2 = shift * (vv1 - 1.0) + (a0 * a0 * h[1] + 2 * a0 * a1 * h[2] + a1 * a1 * h[3])
    q = (-e2 * a0, a0 - e2 * a1, a1)

    def form(offset):
        squares = sum(q[i] * q[i] * h[2 * i + offset] for i in range(3))
        cross = sum(q[i] * q[j] * h[i + j + offset] for i in range(3) for j in range(i))
        return squares + 2 * cross

    rr2 = jnp.maximum(form(0), 0.0)
    rn2 = jnp.sqrt(rr2 + eps)
    c2 = form(1) / (rn2 * rn2) - shift * (eps / (rn2 * rn2))
    gap = (e2 - c2) / 2
    low2 = (e2 + c2) / 2 - jnp.sqrt(gap * gap + rn2 * rn2)
    second = low2 - e2
    g2 = jnp.sqrt(rn2 * rn2 + second * second)
    keep = rn2 / g2
    take = second / (g2 * rn2)
    vector = (
        (keep * a0 + take * q[0]) * b0
        + (keep * a1 + take * q[1]) * b1
        + (take * q[2]) * b2
    )
    return vector, e + rho * low2


def shards(
    psi_start, kept_sizes, left_diag, left_hop, left_hop_dn, right_diag, right_hop, right_hop_dn
):
    width = psi_start.shape[-1]
    count = lax.axis_size("blk")
    sections = lax.axis_size("sect")
    stride = max(2, count // 8)
    up_pairs, dn_pairs = chain(count, stride)
    kept_count = kept_sizes[0, 0]
    row_index = lax.broadcasted_iota(jnp.int32, (width, width), 0)
    col_index = lax.broadcasted_iota(jnp.int32, (width, width), 1)
    kept_mask = (row_index < kept_count) & (col_index < kept_count)
    diag_right = right_diag[0, 0]
    hop_right = right_hop[0, 0]
    hopdn_right = right_hop_dn[0, 0]

    def base_operator(y, diag_left, hop_left, hopdn_left):
        lower_dn = lax.ppermute(y, "blk", dn_pairs)
        lower = lax.ppermute(y, "blk", up_pairs)
        sent_dn = backward_pair(hopdn_left, y, hopdn_right)
        upper_dn = lax.ppermute(sent_dn, "blk", flipped(dn_pairs))
        sent = backward_pair(hop_left, y, hop_right)
        upper = lax.ppermute(sent, "blk", flipped(up_pairs))
        result = forward_pair(diag_left, y, diag_right)
        result = result + forward_pair(hopdn_left, lower_dn, hopdn_right)
        result = result + forward_pair(hop_left, lower, hop_right)
        return result + upper + upper_dn

    def base_expectation(y, diag_left, hop_left, hopdn_left):
        lower_dn = lax.ppermute(y, "blk", dn_pairs)
        lower = lax.ppermute(y, "blk", up_pairs)
        local = forward_pair(diag_left, y, diag_right)
        hops = forward_pair(hop_left, lower, hop_right)
        hops = hops + forward_pair(hopdn_left, lower_dn, hopdn_right)
        return dot(y, local + 2 * hops)

    lefts = (left_diag[0, 0], left_hop[0, 0], left_hop_dn[0, 0])
    to_next = [(s, s + 1) for s in range(sections - 1)]
    first_section = lax.axis_index("sect") == 0
    lefts_next = tuple(
        jnp.where(first_section, own, lax.ppermute(own, "sect", to_next)) for own in lefts
    )

    start = jnp.where(kept_mask, psi_start[0, 0], 0.0)
    vector, _ = krylov_step(
        start * 2.0**-14,
        True,
        lambda x: jnp.where(kept_mask, base_operator(x, *lefts), 0.0),
        lambda x: base_expectation(x, *lefts),
    )

    identity = (row_index == col_index).astype(jnp.float32)
    frame = jnp.where(first_section, identity, lax.ppermute(vector, "sect", to_next))
    env_scale = jnp.where(first_section, 1.0, float(count * width))

    def into(x):
        return jnp.einsum("ab,bc->ac", frame, x, precision=high)

    def operator(x):
        image = base_operator(into(x), *lefts_next)
        image = env_scale * jnp.einsum("ba,bc->ac", frame, image, precision=high)
        return jnp.where(kept_mask, image, 0.0)

    vector, energy = krylov_step(
        vector, False, operator, lambda x: env_scale * base_expectation(into(x), *lefts_next)
    )
    return (vector[None, None], jnp.reshape(energy, (1,)))


def solution(mesh):
    in_specs = (
        P("sect", "blk", None, None),
        P("sect", "blk"),
        P("sect", "blk", None, None, None),
        P("sect", "blk", None, None, None),
        P("sect", "blk", None, None, None),
        P("sect", "blk", None, None, None),
        P("sect", "blk", None, None, None),
        P("sect", "blk", None, None, None),
    )
    out_specs = (P("sect", "blk", None, None), P("sect"))
    return jax.shard_map(shards, mesh=mesh, in_specs=in_specs, out_specs=out_specs, check_vma=False)
```

```python
import jax
import jax.numpy as jnp
from jax import lax
from jax.experimental import pallas as pl
from jax.experimental.pallas import tpu as pltpu
from jax.sharding import PartitionSpec as P

high = lax.Precision.HIGH
EPS = 1e-12
TINY = 1e-6
LIFT = 2048.0
VMEM = pl.BlockSpec(memory_space=pltpu.VMEM)


def chain(count, stride):
    ups = [(k, k + 1) for k in range(count - 1) if (k + 1) % stride != 0]
    downs = [(k, k + stride) for k in range(count - stride)]
    return ups, downs


def flipped(pairs):
    return [(target, source) for source, target in pairs]


def powers(ratio):
    row = lax.broadcasted_iota(jnp.int32, ratio.shape, 0) % 8
    result = jnp.ones_like(ratio)
    for _ in range(5):
        result = jnp.where(row > _, result * ratio, result)
    return result


def merged(tiles):
    unit = tiles[0][8:]
    for tile in tiles[1:]:
        unit = jnp.maximum(unit, tile[8:])
    terms = [tile[:8] * powers(tile[8:] / unit) for tile in tiles]
    while len(terms) > 1:
        terms = [a + b for a, b in zip(terms[::2], terms[1::2])]
    return jnp.concatenate([terms[0], unit], axis=0)


def total(tile):
    count = lax.axis_size("blk")
    step = 1
    while step < count:
        radix = 4 if step * 4 <= count else 2
        tiles = [tile] + [
            lax.ppermute(tile, "blk", [(k, k ^ (step * other)) for k in range(count)])
            for other in range(1, radix)
        ]
        tile = merged(tiles)
        step *= radix
    return tile


def gram_kernel(p_ref, w1_ref, w2_ref, y_ref, image_ref, scale_ref, tile_ref):
    p, w1, w2 = p_ref[...], w1_ref[...], w2_ref[...]

    def peak(x):
        return jnp.max(jnp.max(jnp.abs(x), axis=0, keepdims=True), axis=1, keepdims=True)

    def dot(a, b):
        return jnp.sum(jnp.sum(a * b, axis=0, keepdims=True), axis=1, keepdims=True)

    unit = jnp.maximum(jnp.maximum(peak(w1), jnp.sqrt(peak(w2))), TINY)
    inv = 1.0 / unit
    u1 = w1 * inv
    u2 = w2 * inv * inv
    y = y_ref[...] * inv * inv
    image = image_ref[...] * inv * inv * inv * scale_ref[0:1, 0:1]
    sums = [dot(p, p), dot(p, u1), dot(u1, u1), dot(u1, u2), dot(u2, u2), dot(y, image)]
    row = lax.broadcasted_iota(jnp.int32, (8, 128), 0)
    tile = jnp.zeros((8, 128), jnp.float32)
    for index, value in enumerate(sums):
        tile = jnp.where(row == index, value, tile)
    tile_ref[0:8, :] = tile
    tile_ref[8:16, :] = jnp.broadcast_to(unit, (8, 128))


def finish_kernel(normalise, lift, tile_ref, p_ref, w1_ref, w2_ref, vector_ref, energy_ref):
    unit = tile_ref[8:9, :]
    s = [tile_ref[j : j + 1, :] for j in range(6)]
    norm_sq = s[0] if normalise else jnp.full_like(unit, LIFT * LIFT)
    s = [value / norm_sq for value in s]
    e = s[1]
    h = []
    for j in range(6):
        term = s[j]
        choose = 1
        power = jnp.ones_like(e)
        for i in range(1, j + 1):
            choose = choose * (j - i + 1) // i
            power = power * (-e)
            term = term + float(choose) * power * s[j - i]
        h.append(term)
    h[2] = jnp.maximum(h[2], 0.0)
    eps = EPS / unit / unit
    rn = jnp.sqrt(h[2] + eps)
    c = h[3] / (rn * rn) - e * (eps / (rn * rn))
    low = c / 2 - jnp.sqrt((c / 2) * (c / 2) + rn * rn)
    g = jnp.sqrt(rn * rn + low * low)
    a0 = rn / g
    a1 = low / (g * rn)
    vv1 = a0 * a0 * h[0] + 2 * a0 * a1 * h[1] + a1 * a1 * h[2]
    e2 = e * (vv1 - 1.0) + (a0 * a0 * h[1] + 2 * a0 * a1 * h[2] + a1 * a1 * h[3])
    q = (-e2 * a0, a0 - e2 * a1, a1)

    def form(offset):
        squares = sum(q[i] * q[i] * h[2 * i + offset] for i in range(3))
        cross = sum(q[i] * q[j] * h[i + j + offset] for i in range(3) for j in range(i))
        return squares + 2 * cross

    rn2 = jnp.sqrt(jnp.maximum(form(0), 0.0) + eps)
    c2 = form(1) / (rn2 * rn2) - e * (eps / (rn2 * rn2))
    gap = (e2 - c2) / 2
    low2 = (e2 + c2) / 2 - jnp.sqrt(gap * gap + rn2 * rn2)
    second = low2 - e2
    g2 = jnp.sqrt(rn2 * rn2 + second * second)
    keep = rn2 / g2
    take = second / (g2 * rn2)
    c0, c1, c2 = (keep * a0 + take * q[0], keep * a1 + take * q[1], take * q[2])
    size = lift / jnp.sqrt(norm_sq)
    d0 = (c0 - e * c1 + e * e * c2) * size
    d1 = (c1 - 2 * e * c2) * size / unit
    d2 = c2 * size / unit / unit
    vector_ref[...] = (
        d0[:, 0:1] * p_ref[...] + d1[:, 0:1] * w1_ref[...] + d2[:, 0:1] * w2_ref[...]
    )
    energy_ref[...] = jnp.broadcast_to(unit * (e + low2), (8, 128))


def gram(*operands):
    return pl.pallas_call(
        gram_kernel,
        out_shape=jax.ShapeDtypeStruct((16, 128), jnp.float32),
        in_specs=[VMEM] * 6,
        out_specs=VMEM,
        name="gram",
    )(*operands)


def finish(normalise, lift, tile, p, w1, w2):
    vector, energy = pl.pallas_call(
        lambda *refs: finish_kernel(normalise, lift, *refs),
        out_shape=(
            jax.ShapeDtypeStruct(p.shape, jnp.float32),
            jax.ShapeDtypeStruct((8, 128), jnp.float32),
        ),
        in_specs=[VMEM] * 4,
        out_specs=(VMEM, VMEM),
        name="finish",
    )(tile, p, w1, w2)
    return vector, energy[0, 0]


def forward_pair(left_env, state_block, right_env):
    inner_term = jnp.einsum("wab,bc->wac", left_env, state_block, precision=high)
    return jnp.einsum("wac,wdc->ad", inner_term, right_env, precision=high)


def backward_pair(left_env, state_block, right_env):
    inner_term = jnp.einsum("wba,bc->wac", left_env, state_block, precision=high)
    return jnp.einsum("wac,wcd->ad", inner_term, right_env, precision=high)


def shards(
    psi_start, kept_sizes, left_diag, left_hop, left_hop_dn, right_diag, right_hop, right_hop_dn
):
    width = psi_start.shape[-1]
    count = lax.axis_size("blk")
    sections = lax.axis_size("sect")
    stride = max(2, count // 8)
    up_pairs, dn_pairs = chain(count, stride)
    kept_count = kept_sizes[0, 0]
    row_index = lax.broadcasted_iota(jnp.int32, (width, width), 0)
    col_index = lax.broadcasted_iota(jnp.int32, (width, width), 1)
    kept_mask = (row_index < kept_count) & (col_index < kept_count)
    diag_right = right_diag[0, 0]
    hop_right = right_hop[0, 0]
    hopdn_right = right_hop_dn[0, 0]

    def base_operator(y, diag_left, hop_left, hopdn_left):
        lower_dn = lax.ppermute(y, "blk", dn_pairs)
        lower = lax.ppermute(y, "blk", up_pairs)
        sent_dn = backward_pair(hopdn_left, y, hopdn_right)
        upper_dn = lax.ppermute(sent_dn, "blk", flipped(dn_pairs))
        sent = backward_pair(hop_left, y, hop_right)
        upper = lax.ppermute(sent, "blk", flipped(up_pairs))
        result = forward_pair(diag_left, y, diag_right)
        result = result + forward_pair(hopdn_left, lower_dn, hopdn_right)
        result = result + forward_pair(hop_left, lower, hop_right)
        return result + upper + upper_dn

    def half_image(y, diag_left, hop_left, hopdn_left):
        lower_dn = lax.ppermute(y, "blk", dn_pairs)
        lower = lax.ppermute(y, "blk", up_pairs)
        local = forward_pair(diag_left, y, diag_right)
        hops = forward_pair(hop_left, lower, hop_right)
        hops = hops + forward_pair(hopdn_left, lower_dn, hopdn_right)
        return local + 2 * hops

    lefts = (left_diag[0, 0], left_hop[0, 0], left_hop_dn[0, 0])
    to_next = [(s, s + 1) for s in range(sections - 1)]
    first_section = lax.axis_index("sect") == 0
    lefts_next = tuple(
        jnp.where(first_section, own, lax.ppermute(own, "sect", to_next)) for own in lefts
    )

    p = jnp.where(kept_mask, psi_start[0, 0], 0.0)
    w1 = jnp.where(kept_mask, base_operator(p, *lefts), 0.0)
    w2 = jnp.where(kept_mask, base_operator(w1, *lefts), 0.0)
    one = jnp.ones((8, 128), jnp.float32)
    tile = total(gram(p, w1, w2, w2, half_image(w2, *lefts), one))
    vector, _ = finish(True, LIFT, tile, p, w1, w2)

    identity = (row_index == col_index).astype(jnp.float32)
    received = lax.ppermute(vector, "sect", to_next) * (1.0 / LIFT)
    frame = jnp.where(first_section, identity, received)
    env_scale = jnp.where(first_section, 1.0, float(count * width))

    def into(x):
        return jnp.einsum("ab,bc->ac", frame, x, precision=high)

    def operator(y):
        image = base_operator(y, *lefts_next)
        image = env_scale * jnp.einsum("ba,bc->ac", frame, image, precision=high)
        return jnp.where(kept_mask, image, 0.0)

    p = vector
    w1 = operator(into(p))
    w2 = operator(into(w1))
    y = into(w2)
    tile = total(gram(p, w1, w2, y, half_image(y, *lefts_next), one * env_scale))
    vector, energy = finish(False, 1.0, tile, p, w1, w2)
    return (vector[None, None], jnp.reshape(energy, (1,)))


def solution(mesh):
    in_specs = (
        P("sect", "blk", None, None),
        P("sect", "blk"),
        P("sect", "blk", None, None, None),
        P("sect", "blk", None, None, None),
        P("sect", "blk", None, None, None),
        P("sect", "blk", None, None, None),
        P("sect", "blk", None, None, None),
        P("sect", "blk", None, None, None),
    )
    out_specs = (P("sect", "blk", None, None), P("sect"))
    return jax.shard_map(shards, mesh=mesh, in_specs=in_specs, out_specs=out_specs, check_vma=False)
```

```python
import functools

import jax
import jax.numpy as jnp
from jax import lax
from jax.experimental import pallas as pl
from jax.experimental.pallas import tpu as pltpu
from jax.sharding import PartitionSpec as P

high = lax.Precision.HIGH
EPS = 1e-12
TINY = 1e-6
LIFT = 2048.0
ROOM = 32 * 2**20
VMEM = pl.BlockSpec(memory_space=pltpu.VMEM)


def chain(count, stride):
    ups = [(k, k + 1) for k in range(count - 1) if (k + 1) % stride != 0]
    downs = [(k, k + stride) for k in range(count - stride)]
    return ups, downs


def flipped(pairs):
    return [(target, source) for source, target in pairs]


def merged(tiles):
    tiles = list(tiles)
    while len(tiles) > 1:
        tiles = [a + b for a, b in zip(tiles[::2], tiles[1::2])]
    return tiles[0]


def lane_units():
    group = lax.broadcasted_iota(jnp.int32, (1, 128), 1) // 16
    unit = jnp.full((1, 128), 2.0**-48, jnp.float32)
    for index in range(1, 8):
        unit = jnp.where(group == index, 2.0 ** (16 * index - 48), unit)
    return group, unit


def spread(tile):
    count = lax.axis_size("blk")
    step = 1
    tiles = [tile]
    while step < count:
        radix = 4 if step * 4 <= count else 2
        tile = merged(tiles) if len(tiles) > 1 else tiles[0]
        tiles = [tile] + [
            lax.ppermute(tile, "blk", [(k, k ^ (step * other)) for k in range(count)])
            for other in range(1, radix)
        ]
        step *= radix
    return tiles


def dot(a, b):
    return jnp.sum(jnp.sum(a * b, axis=0, keepdims=True), axis=1, keepdims=True)


def peak(x):
    return jnp.max(jnp.max(jnp.abs(x), axis=0, keepdims=True), axis=1, keepdims=True)


def factor(env_scale, first_ref):
    return jnp.where(first_ref[0] == 1, 1.0, env_scale)


def gram_tile(p, w1, w2, y, local, scale):
    unit = jnp.maximum(jnp.maximum(peak(w1), jnp.sqrt(peak(w2))), TINY)
    inv = 1.0 / unit
    u1 = w1 * inv
    u2 = w2 * inv * inv
    y = y * inv * inv
    local = local * inv * inv * inv * scale
    sums = [dot(p, p), dot(p, u1), dot(u1, u1), dot(u1, u2), dot(u2, u2), dot(y, local)]
    row = lax.broadcasted_iota(jnp.int32, (8, 128), 0)
    tile = jnp.broadcast_to(unit, (8, 128))
    for index, value in enumerate(sums):
        tile = jnp.where(row == index, value, tile)
    return tile


def hops_kernel(env_scale, tile_ref, sent_ref, got_ref, sent_dn_ref, got_dn_ref, first_ref, out_ref):
    tile = tile_ref[...]
    inv = 1.0 / tile[7:8, 0:1]
    size = inv * inv * inv * (2 * factor(env_scale, first_ref))
    both = (sent_ref[...] * size) * (got_ref[...] * inv * inv)
    both = both + (sent_dn_ref[...] * size) * (got_dn_ref[...] * inv * inv)
    row = lax.broadcasted_iota(jnp.int32, (8, 128), 0)
    both = jnp.sum(jnp.sum(both, axis=0, keepdims=True), axis=1, keepdims=True)
    tile = jnp.where(row == 5, tile + both, tile)
    ratio = tile[7:8, :] / lane_units()[1]
    for power in range(1, 6):
        tile = jnp.where((row >= power) & (row < 6), tile * ratio, tile)
    out_ref[...] = tile


def finish_kernel(normalise, lift, *refs):
    *tile_refs, p_ref, w1_ref, w2_ref, vector_ref, energy_ref = refs
    tile = merged([ref[...] for ref in tile_refs])
    group, unit = lane_units()
    s = [tile[j : j + 1, :] for j in range(6)]
    norm_sq = s[0] if normalise else jnp.full_like(unit, LIFT * LIFT)
    s = [value / norm_sq for value in s]
    fits = ((s[2] >= 2.0**-16) | (group == 0)) & ((s[2] < 2.0**16) | (group == 7))
    e = s[1]
    h = []
    for j in range(6):
        term = s[j]
        choose = 1
        power = jnp.ones_like(e)
        for i in range(1, j + 1):
            choose = choose * (j - i + 1) // i
            power = power * (-e)
            term = term + float(choose) * power * s[j - i]
        h.append(term)
    h[2] = jnp.maximum(h[2], 0.0)
    eps = EPS / unit / unit
    rn = jnp.sqrt(h[2] + eps)
    c = h[3] / (rn * rn) - e * (eps / (rn * rn))
    low = c / 2 - jnp.sqrt((c / 2) * (c / 2) + rn * rn)
    g = jnp.sqrt(rn * rn + low * low)
    a0 = rn / g
    a1 = low / (g * rn)
    vv1 = a0 * a0 * h[0] + 2 * a0 * a1 * h[1] + a1 * a1 * h[2]
    e2 = e * (vv1 - 1.0) + (a0 * a0 * h[1] + 2 * a0 * a1 * h[2] + a1 * a1 * h[3])
    q = (-e2 * a0, a0 - e2 * a1, a1)

    def form(offset):
        squares = sum(q[i] * q[i] * h[2 * i + offset] for i in range(3))
        cross = sum(q[i] * q[j] * h[i + j + offset] for i in range(3) for j in range(i))
        return squares + 2 * cross

    rn2 = jnp.sqrt(jnp.maximum(form(0), 0.0) + eps)
    c2 = form(1) / (rn2 * rn2) - e * (eps / (rn2 * rn2))
    gap = (e2 - c2) / 2
    low2 = (e2 + c2) / 2 - jnp.sqrt(gap * gap + rn2 * rn2)
    second = low2 - e2
    g2 = jnp.sqrt(rn2 * rn2 + second * second)
    keep = rn2 / g2
    take = second / (g2 * rn2)
    c0, c1, c2 = (keep * a0 + take * q[0], keep * a1 + take * q[1], take * q[2])
    size = lift / jnp.sqrt(norm_sq)
    d0 = (c0 - e * c1 + e * e * c2) * size
    d1 = (c1 - 2 * e * c2) * size / unit
    d2 = c2 * size / unit / unit

    def pick(value):
        return jnp.max(jnp.where(fits, value, -jnp.inf), axis=1, keepdims=True)

    d0, d1, d2 = pick(d0), pick(d1), pick(d2)
    vector_ref[...] = d0 * p_ref[...] + d1 * w1_ref[...] + d2 * w2_ref[...]
    energy_ref[0] = pick(unit * (e + low2))[0, 0]


SMEM = pl.BlockSpec(memory_space=pltpu.SMEM)
CHEAP = pl.CostEstimate(flops=1, bytes_accessed=1, transcendentals=0)
TILE = jax.ShapeDtypeStruct((8, 128), jnp.float32)


def moments_kernel(env_scale, *refs):
    y_ref, p_ref, w1_ref, w2_ref, ln, rn, lh, rh, ld, rd, first_ref = refs[:11]
    dn_ref, up_ref, tile_ref, local_ref = refs[11:]
    step = pl.program_id(0)
    parts = split(y_ref[...])
    terms = (
        pair_term(False, ln[0], rn[0], parts),
        pair_term(False, lh[0], rh[0], parts),
        pair_term(True, ld[0], rd[0], parts),
    )

    @pl.when(step == 0)
    def _():
        for ref, term in zip((dn_ref, up_ref, local_ref), terms):
            ref[...] = term

    @pl.when(step > 0)
    def _():
        for ref, term in zip((dn_ref, up_ref, local_ref), terms):
            ref[...] += term

    @pl.when(step == pl.num_programs(0) - 1)
    def _():
        tile_ref[...] = gram_tile(
            p_ref[...], w1_ref[...], w2_ref[...], y_ref[...], local_ref[...],
            factor(env_scale, first_ref),
        )


def first_moments(env_scale, first, y, p, w1, w2, envs):
    channels, width, _ = envs[0].shape
    whole = pl.BlockSpec((width, width), lambda w: (0, 0))
    env = pl.BlockSpec((1, width, width), lambda w: (w, 0, 0))
    block = jax.ShapeDtypeStruct((width, width), jnp.float32)
    return pl.pallas_call(
        functools.partial(moments_kernel, env_scale),
        grid=(channels,),
        out_shape=(block, block, TILE),
        in_specs=[whole] * 4 + [env] * 6 + [SMEM],
        out_specs=(whole, whole, pl.BlockSpec((8, 128), lambda w: (0, 0))),
        scratch_shapes=[pltpu.VMEM((width, width), jnp.float32)],
        compiler_params=pltpu.CompilerParams(vmem_limit_bytes=ROOM),
        cost_estimate=CHEAP,
        name="moments",
    )(y, p, w1, w2, *envs, first)


def add_hops(env_scale, first, tile, sent, got, sent_dn, got_dn):
    return pl.pallas_call(
        functools.partial(hops_kernel, env_scale),
        out_shape=TILE,
        in_specs=[VMEM] * 5 + [SMEM],
        out_specs=VMEM,
        cost_estimate=CHEAP,
        name="add_hops",
    )(tile, sent, got, sent_dn, got_dn, first)


def finish(normalise, lift, tiles, p, w1, w2):
    return pl.pallas_call(
        functools.partial(finish_kernel, normalise, lift),
        out_shape=(
            jax.ShapeDtypeStruct(p.shape, jnp.float32),
            jax.ShapeDtypeStruct((1,), jnp.float32),
        ),
        in_specs=[VMEM] * (len(tiles) + 3),
        out_specs=(VMEM, SMEM),
        cost_estimate=CHEAP,
        name="finish",
    )(*tiles, p, w1, w2)


def forward_pair(left_env, state_block, right_env):
    inner_term = jnp.einsum("wab,bc->wac", left_env, state_block, precision=high)
    return jnp.einsum("wac,wdc->ad", inner_term, right_env, precision=high)


def backward_pair(left_env, state_block, right_env):
    inner_term = jnp.einsum("wba,bc->wac", left_env, state_block, precision=high)
    return jnp.einsum("wac,wcd->ad", inner_term, right_env, precision=high)


def split(x):
    top = x.astype(jnp.bfloat16)
    return top, (x - top.astype(jnp.float32)).astype(jnp.bfloat16)


def product(a, b, flip=False):
    dims = (((1,), (1 if flip else 0,)), ((), ()))

    def one(x, y):
        return lax.dot_general(x, y, dims, preferred_element_type=jnp.float32)

    (a0, a1), (b0, b1) = a, b
    return one(a0, b0) + (one(a0, b1) + one(a1, b0))


def pair_term(forward, left, right, x):
    if forward:
        return product(split(product(split(left), x)), split(right), flip=True)
    return product(split(product(split(left.T), x)), split(right))


def shards(
    psi_start, kept_sizes, left_diag, left_hop, left_hop_dn, right_diag, right_hop, right_hop_dn
):
    width = psi_start.shape[-1]
    count = lax.axis_size("blk")
    sections = lax.axis_size("sect")
    stride = max(2, count // 8)
    up_pairs, dn_pairs = chain(count, stride)
    kept_count = kept_sizes[0, 0]
    row_index = lax.broadcasted_iota(jnp.int32, (width, width), 0)
    col_index = lax.broadcasted_iota(jnp.int32, (width, width), 1)
    kept_mask = (row_index < kept_count) & (col_index < kept_count)
    diag_right = right_diag[0, 0]
    hop_right = right_hop[0, 0]
    hopdn_right = right_hop_dn[0, 0]

    def base_operator(y, lefts, extra=()):
        diag_left, hop_left, hopdn_left = lefts
        lower_dn = lax.ppermute(y, "blk", dn_pairs)
        sent_dn = backward_pair(hopdn_left, y, hopdn_right)
        upper_dn = lax.ppermute(sent_dn, "blk", flipped(dn_pairs))
        lower = lax.ppermute(y, "blk", up_pairs)
        sent = backward_pair(hop_left, y, hop_right)
        upper = lax.ppermute(sent, "blk", flipped(up_pairs))
        image = forward_pair(diag_left, y, diag_right)
        image = image + forward_pair(hopdn_left, lower_dn, hopdn_right)
        image = image + forward_pair(hop_left, lower, hop_right)
        image, extra = lax.optimization_barrier((image, extra))
        return image + upper + upper_dn, extra

    def moments(env_scale, p, w1, w2, y, lefts, extra=()):
        diag_left, hop_left, hopdn_left = lefts
        envs = (hopdn_left, hopdn_right, hop_left, hop_right, diag_left, diag_right)
        got_dn = lax.ppermute(y, "blk", dn_pairs)
        sent_dn, sent, tile = first_moments(env_scale, first, y, p, w1, w2, envs)
        got = lax.ppermute(y, "blk", up_pairs)
        tile, extra = lax.optimization_barrier((tile, extra))
        return spread(add_hops(env_scale, first, tile, sent, got, sent_dn, got_dn)), extra

    lefts = (left_diag[0, 0], left_hop[0, 0], left_hop_dn[0, 0])
    to_next = [(s, s + 1) for s in range(sections - 1)]
    first_section = lax.axis_index("sect") == 0
    env_scale = float(count * width)
    env_factor = jnp.where(first_section, 1.0, env_scale)

    moved = [lax.ppermute(own, "sect", to_next) for own in lefts]

    def chosen(index):
        return jnp.where(first_section, lefts[index], moved[index])

    first = jnp.reshape(first_section.astype(jnp.int32), (1,))
    p = jnp.where(kept_mask, psi_start[0, 0], 0.0)
    w1, _ = base_operator(p, lefts)
    w1 = jnp.where(kept_mask, w1, 0.0)
    w2, hopdn_next = base_operator(w1, lefts, chosen(2))
    w2 = jnp.where(kept_mask, w2, 0.0)
    tiles, hop_next = moments(1.0, p, w1, w2, w2, lefts, chosen(1))
    tiles, diag_next = lax.optimization_barrier((tiles, chosen(0)))
    lefts_next = (diag_next, hop_next, hopdn_next)
    vector, _ = finish(True, LIFT, tiles, p, w1, w2)

    identity = (row_index == col_index).astype(jnp.float32)
    received = lax.ppermute(vector, "sect", to_next) * (1.0 / LIFT)
    frame = jnp.where(first_section, identity, received)

    def into(x):
        return jnp.einsum("ab,bc->ac", frame, x, precision=high)

    def operator(y):
        image, _ = base_operator(y, lefts_next)
        image = jnp.einsum("ba,bc->ac", frame, image, precision=high)
        image = env_factor * image
        return jnp.where(kept_mask, image, 0.0)

    p = vector
    w1 = operator(into(p))
    w2 = operator(into(w1))
    tiles, _ = moments(env_scale, p, w1, w2, into(w2), lefts_next)
    vector, energy = finish(False, 1.0, tiles, p, w1, w2)
    return (vector[None, None], energy)


def solution(mesh):
    in_specs = (
        P("sect", "blk", None, None),
        P("sect", "blk"),
        P("sect", "blk", None, None, None),
        P("sect", "blk", None, None, None),
        P("sect", "blk", None, None, None),
        P("sect", "blk", None, None, None),
        P("sect", "blk", None, None, None),
        P("sect", "blk", None, None, None),
    )
    out_specs = (P("sect", "blk", None, None), P("sect"))
    return jax.shard_map(shards, mesh=mesh, in_specs=in_specs, out_specs=out_specs, check_vma=False)
```

```python
import functools

import jax
import jax.numpy as jnp
from jax import lax
from jax.experimental import pallas as pl
from jax.experimental.pallas import tpu as pltpu
from jax.sharding import PartitionSpec as P

high = lax.Precision.HIGH
EPS = 1e-12
TINY = 1e-6
LIFT = 2048.0
ROOM = 32 * 2**20
VMEM = pl.BlockSpec(memory_space=pltpu.VMEM)


def chain(count, stride):
    ups = [(k, k + 1) for k in range(count - 1) if (k + 1) % stride != 0]
    downs = [(k, k + stride) for k in range(count - stride)]
    return ups, downs


def flipped(pairs):
    return [(target, source) for source, target in pairs]


def merged(tiles):
    tiles = list(tiles)
    while len(tiles) > 1:
        tiles = [a + b for a, b in zip(tiles[::2], tiles[1::2])]
    return tiles[0]


def lane_units():
    group = lax.broadcasted_iota(jnp.int32, (1, 128), 1) // 16
    unit = jnp.full((1, 128), 2.0**-48, jnp.float32)
    for index in range(1, 8):
        unit = jnp.where(group == index, 2.0 ** (16 * index - 48), unit)
    return group, unit


def spread(tile):
    count = lax.axis_size("blk")
    step = 1
    tiles = [tile]
    while step < count:
        radix = 4 if step * 4 <= count else 2
        tile = merged(tiles) if len(tiles) > 1 else tiles[0]
        tiles = [tile] + [
            lax.ppermute(tile, "blk", [(k, k ^ (step * other)) for k in range(count)])
            for other in range(1, radix)
        ]
        step *= radix
    return tiles


def dot(a, b):
    return jnp.sum(jnp.sum(a * b, axis=0, keepdims=True), axis=1, keepdims=True)


def peak(x):
    return jnp.max(jnp.max(jnp.abs(x), axis=0, keepdims=True), axis=1, keepdims=True)


def factor(env_scale, first_ref):
    return jnp.where(first_ref[0] == 1, 1.0, env_scale)


def gram_tile(p, w1, w2, y, local, scale):
    unit = jnp.maximum(jnp.maximum(peak(w1), jnp.sqrt(peak(w2))), TINY)
    inv = 1.0 / unit
    u1 = w1 * inv
    u2 = w2 * inv * inv
    y = y * inv * inv
    local = local * inv * inv * inv * scale
    sums = [dot(p, p), dot(p, u1), dot(u1, u1), dot(u1, u2), dot(u2, u2), dot(y, local)]
    row = lax.broadcasted_iota(jnp.int32, (8, 128), 0)
    tile = jnp.broadcast_to(unit, (8, 128))
    for index, value in enumerate(sums):
        tile = jnp.where(row == index, value, tile)
    return tile


def hops_kernel(env_scale, tile_ref, sent_ref, got_ref, sent_dn_ref, got_dn_ref, first_ref, out_ref):
    tile = tile_ref[...]
    inv = 1.0 / tile[7:8, 0:1]
    size = inv * inv * inv * (2 * factor(env_scale, first_ref))
    both = (sent_ref[...] * size) * (got_ref[...] * inv * inv)
    both = both + (sent_dn_ref[...] * size) * (got_dn_ref[...] * inv * inv)
    row = lax.broadcasted_iota(jnp.int32, (8, 128), 0)
    both = jnp.sum(jnp.sum(both, axis=0, keepdims=True), axis=1, keepdims=True)
    tile = jnp.where(row == 5, tile + both, tile)
    ratio = tile[7:8, :] / lane_units()[1]
    for power in range(1, 6):
        tile = jnp.where((row >= power) & (row < 6), tile * ratio, tile)
    out_ref[...] = tile


def finish_kernel(normalise, lift, *refs):
    *tile_refs, p_ref, w1_ref, w2_ref, vector_ref, energy_ref = refs
    tile = merged([ref[...] for ref in tile_refs])
    group, unit = lane_units()
    s = [tile[j : j + 1, :] for j in range(6)]
    norm_sq = s[0] if normalise else jnp.full_like(unit, LIFT * LIFT)
    s = [value / norm_sq for value in s]
    fits = ((s[2] >= 2.0**-16) | (group == 0)) & ((s[2] < 2.0**16) | (group == 7))
    e = s[1]
    h = []
    for j in range(6):
        term = s[j]
        choose = 1
        power = jnp.ones_like(e)
        for i in range(1, j + 1):
            choose = choose * (j - i + 1) // i
            power = power * (-e)
            term = term + float(choose) * power * s[j - i]
        h.append(term)
    h[2] = jnp.maximum(h[2], 0.0)
    eps = EPS / unit / unit
    rn = jnp.sqrt(h[2] + eps)
    c = h[3] / (rn * rn) - e * (eps / (rn * rn))
    low = c / 2 - jnp.sqrt((c / 2) * (c / 2) + rn * rn)
    g = jnp.sqrt(rn * rn + low * low)
    a0 = rn / g
    a1 = low / (g * rn)
    vv1 = a0 * a0 * h[0] + 2 * a0 * a1 * h[1] + a1 * a1 * h[2]
    e2 = e * (vv1 - 1.0) + (a0 * a0 * h[1] + 2 * a0 * a1 * h[2] + a1 * a1 * h[3])
    q = (-e2 * a0, a0 - e2 * a1, a1)

    def form(offset):
        squares = sum(q[i] * q[i] * h[2 * i + offset] for i in range(3))
        cross = sum(q[i] * q[j] * h[i + j + offset] for i in range(3) for j in range(i))
        return squares + 2 * cross

    rn2 = jnp.sqrt(jnp.maximum(form(0), 0.0) + eps)
    c2 = form(1) / (rn2 * rn2) - e * (eps / (rn2 * rn2))
    gap = (e2 - c2) / 2
    low2 = (e2 + c2) / 2 - jnp.sqrt(gap * gap + rn2 * rn2)
    second = low2 - e2
    g2 = jnp.sqrt(rn2 * rn2 + second * second)
    keep = rn2 / g2
    take = second / (g2 * rn2)
    c0, c1, c2 = (keep * a0 + take * q[0], keep * a1 + take * q[1], take * q[2])
    size = lift / jnp.sqrt(norm_sq)
    d0 = (c0 - e * c1 + e * e * c2) * size
    d1 = (c1 - 2 * e * c2) * size / unit
    d2 = c2 * size / unit / unit

    def pick(value):
        return jnp.max(jnp.where(fits, value, -jnp.inf), axis=1, keepdims=True)

    d0, d1, d2 = pick(d0), pick(d1), pick(d2)
    vector_ref[...] = d0 * p_ref[...] + d1 * w1_ref[...] + d2 * w2_ref[...]
    energy_ref[0] = pick(unit * (e + low2))[0, 0]


SMEM = pl.BlockSpec(memory_space=pltpu.SMEM)
CHEAP = pl.CostEstimate(flops=1, bytes_accessed=1, transcendentals=0)
TILE = jax.ShapeDtypeStruct((8, 128), jnp.float32)


def moments_kernel(env_scale, *refs):
    y_ref, p_ref, w1_ref, w2_ref, ln, rn, lh, rh, ld, rd, first_ref = refs[:11]
    dn_ref, up_ref, tile_ref, local_ref = refs[11:]
    step = pl.program_id(0)
    parts = split(y_ref[...])
    terms = (
        pair_term(False, ln[0], rn[0], parts),
        pair_term(False, lh[0], rh[0], parts),
        pair_term(True, ld[0], rd[0], parts),
    )

    @pl.when(step == 0)
    def _():
        for ref, term in zip((dn_ref, up_ref, local_ref), terms):
            ref[...] = term

    @pl.when(step > 0)
    def _():
        for ref, term in zip((dn_ref, up_ref, local_ref), terms):
            ref[...] += term

    @pl.when(step == pl.num_programs(0) - 1)
    def _():
        tile_ref[...] = gram_tile(
            p_ref[...], w1_ref[...], w2_ref[...], y_ref[...], local_ref[...],
            factor(env_scale, first_ref),
        )


def first_moments(env_scale, first, y, p, w1, w2, envs):
    channels, width, _ = envs[0].shape
    whole = pl.BlockSpec((width, width), lambda w: (0, 0))
    env = pl.BlockSpec((1, width, width), lambda w: (w, 0, 0))
    block = jax.ShapeDtypeStruct((width, width), jnp.float32)
    return pl.pallas_call(
        functools.partial(moments_kernel, env_scale),
        grid=(channels,),
        out_shape=(block, block, TILE),
        in_specs=[whole] * 4 + [env] * 6 + [SMEM],
        out_specs=(whole, whole, pl.BlockSpec((8, 128), lambda w: (0, 0))),
        scratch_shapes=[pltpu.VMEM((width, width), jnp.float32)],
        compiler_params=pltpu.CompilerParams(vmem_limit_bytes=ROOM),
        cost_estimate=CHEAP,
        name="moments",
    )(y, p, w1, w2, *envs, first)


def add_hops(env_scale, first, tile, sent, got, sent_dn, got_dn):
    return pl.pallas_call(
        functools.partial(hops_kernel, env_scale),
        out_shape=TILE,
        in_specs=[VMEM] * 5 + [SMEM],
        out_specs=VMEM,
        cost_estimate=CHEAP,
        name="add_hops",
    )(tile, sent, got, sent_dn, got_dn, first)


def finish(normalise, lift, tiles, p, w1, w2):
    return pl.pallas_call(
        functools.partial(finish_kernel, normalise, lift),
        out_shape=(
            jax.ShapeDtypeStruct(p.shape, jnp.float32),
            jax.ShapeDtypeStruct((1,), jnp.float32),
        ),
        in_specs=[VMEM] * (len(tiles) + 3),
        out_specs=(VMEM, SMEM),
        cost_estimate=CHEAP,
        name="finish",
    )(*tiles, p, w1, w2)


def forward_pair(left_env, state_block, right_env):
    inner_term = jnp.einsum("wab,bc->wac", left_env, state_block, precision=high)
    return jnp.einsum("wac,wdc->ad", inner_term, right_env, precision=high)


def backward_pair(left_env, state_block, right_env):
    inner_term = jnp.einsum("wba,bc->wac", left_env, state_block, precision=high)
    return jnp.einsum("wac,wcd->ad", inner_term, right_env, precision=high)


def split(x):
    top = x.astype(jnp.bfloat16)
    return top, (x - top.astype(jnp.float32)).astype(jnp.bfloat16)


def product(a, b, flip=False):
    dims = (((1,), (1 if flip else 0,)), ((), ()))

    def one(x, y):
        return lax.dot_general(x, y, dims, preferred_element_type=jnp.float32)

    (a0, a1), (b0, b1) = a, b
    return one(a0, b0) + (one(a0, b1) + one(a1, b0))


def pair_term(forward, left, right, x):
    if forward:
        return product(split(product(split(left), x)), split(right), flip=True)
    return product(split(product(split(left.T), x)), split(right))


def shards(
    psi_start, kept_sizes, left_diag, left_hop, left_hop_dn, right_diag, right_hop, right_hop_dn
):
    width = psi_start.shape[-1]
    count = lax.axis_size("blk")
    sections = lax.axis_size("sect")
    stride = max(2, count // 8)
    up_pairs, dn_pairs = chain(count, stride)
    kept_count = kept_sizes[0, 0]
    row_index = lax.broadcasted_iota(jnp.int32, (width, width), 0)
    col_index = lax.broadcasted_iota(jnp.int32, (width, width), 1)
    kept_mask = (row_index < kept_count) & (col_index < kept_count)
    diag_right = right_diag[0, 0]
    hop_right = right_hop[0, 0]
    hopdn_right = right_hop_dn[0, 0]

    def base_operator(y, lefts, extra=(), tied=False):
        diag_left, hop_left, hopdn_left = lefts
        lower_dn = lax.ppermute(y, "blk", dn_pairs)
        sent_dn = backward_pair(hopdn_left, y, hopdn_right)
        if tied:
            y, sent_dn = lax.optimization_barrier((y, sent_dn))
        upper_dn = lax.ppermute(sent_dn, "blk", flipped(dn_pairs))
        lower = lax.ppermute(y, "blk", up_pairs)
        sent = backward_pair(hop_left, y, hop_right)
        upper = lax.ppermute(sent, "blk", flipped(up_pairs))
        image = forward_pair(diag_left, y, diag_right)
        image = image + forward_pair(hopdn_left, lower_dn, hopdn_right)
        image = image + forward_pair(hop_left, lower, hop_right)
        image, extra = lax.optimization_barrier((image, extra))
        return image + upper + upper_dn, extra

    def moments(env_scale, p, w1, w2, y, lefts, extra=()):
        diag_left, hop_left, hopdn_left = lefts
        envs = (hopdn_left, hopdn_right, hop_left, hop_right, diag_left, diag_right)
        got_dn = lax.ppermute(y, "blk", dn_pairs)
        sent_dn, sent, tile = first_moments(env_scale, first, y, p, w1, w2, envs)
        got = lax.ppermute(y, "blk", up_pairs)
        tile, extra = lax.optimization_barrier((tile, extra))
        return spread(add_hops(env_scale, first, tile, sent, got, sent_dn, got_dn)), extra

    lefts = (left_diag[0, 0], left_hop[0, 0], left_hop_dn[0, 0])
    to_next = [(s, s + 1) for s in range(sections - 1)]
    first_section = lax.axis_index("sect") == 0
    env_scale = float(count * width)
    env_factor = jnp.where(first_section, 1.0, env_scale)

    moved = [lax.ppermute(own, "sect", to_next) for own in lefts]

    def chosen(index):
        return jnp.where(first_section, lefts[index], moved[index])

    first = jnp.reshape(first_section.astype(jnp.int32), (1,))
    p = jnp.where(kept_mask, psi_start[0, 0], 0.0)
    w1, _ = base_operator(p, lefts)
    w1 = jnp.where(kept_mask, w1, 0.0)
    w2, hopdn_next = base_operator(w1, lefts, chosen(2))
    w2 = jnp.where(kept_mask, w2, 0.0)
    tiles, hop_next = moments(1.0, p, w1, w2, w2, lefts, chosen(1))
    tiles, diag_next = lax.optimization_barrier((tiles, chosen(0)))
    lefts_next = (diag_next, hop_next, hopdn_next)
    vector, _ = finish(True, LIFT, tiles, p, w1, w2)

    identity = (row_index == col_index).astype(jnp.float32)
    received = lax.ppermute(vector, "sect", to_next) * (1.0 / LIFT)
    frame = jnp.where(first_section, identity, received)

    def into(x):
        return jnp.einsum("ab,bc->ac", frame, x, precision=high)

    def operator(y, tied):
        image, _ = base_operator(y, lefts_next, tied=tied)
        image = jnp.einsum("ba,bc->ac", frame, image, precision=high)
        image = env_factor * image
        return jnp.where(kept_mask, image, 0.0)

    p = vector
    w1 = operator(into(p), True)
    w2 = operator(into(w1), False)
    tiles, _ = moments(env_scale, p, w1, w2, into(w2), lefts_next)
    vector, energy = finish(False, 1.0, tiles, p, w1, w2)
    return (vector[None, None], energy)


def solution(mesh):
    in_specs = (
        P("sect", "blk", None, None),
        P("sect", "blk"),
        P("sect", "blk", None, None, None),
        P("sect", "blk", None, None, None),
        P("sect", "blk", None, None, None),
        P("sect", "blk", None, None, None),
        P("sect", "blk", None, None, None),
        P("sect", "blk", None, None, None),
    )
    out_specs = (P("sect", "blk", None, None), P("sect"))
    return jax.shard_map(shards, mesh=mesh, in_specs=in_specs, out_specs=out_specs, check_vma=False)
```

```python
import functools

import jax
import jax.numpy as jnp
from jax import lax
from jax.experimental import pallas as pl
from jax.experimental.pallas import tpu as pltpu
from jax.sharding import PartitionSpec as P

high = lax.Precision.HIGH
EPS = 1e-12
TINY = 1e-6
LIFT = 2048.0
ROOM = 32 * 2**20
VMEM = pl.BlockSpec(memory_space=pltpu.VMEM)


def chain(count, stride):
    ups = [(k, k + 1) for k in range(count - 1) if (k + 1) % stride != 0]
    downs = [(k, k + stride) for k in range(count - stride)]
    return ups, downs


def flipped(pairs):
    return [(target, source) for source, target in pairs]


def merged(tiles):
    tiles = list(tiles)
    while len(tiles) > 1:
        tiles = [a + b for a, b in zip(tiles[::2], tiles[1::2])]
    return tiles[0]


def lane_units():
    group = lax.broadcasted_iota(jnp.int32, (1, 128), 1) // 16
    unit = jnp.full((1, 128), 2.0**-48, jnp.float32)
    for index in range(1, 8):
        unit = jnp.where(group == index, 2.0 ** (16 * index - 48), unit)
    return group, unit


def spread(tile):
    count = lax.axis_size("blk")
    step = 1
    stages = []
    while step < count:
        radix = 4 if step * 4 <= count else 2
        stages.append((step, radix))
        step *= radix
    tiles = [tile]
    for step, radix in reversed(stages):
        tile = merged(tiles)
        tiles = [tile] + [
            lax.ppermute(tile, "blk", [(k, k ^ (step * other)) for k in range(count)])
            for other in range(1, radix)
        ]
    return tiles


def dot(a, b):
    return jnp.sum(jnp.sum(a * b, axis=0, keepdims=True), axis=1, keepdims=True)


def peak(x):
    return jnp.max(jnp.max(jnp.abs(x), axis=0, keepdims=True), axis=1, keepdims=True)


def factor(env_scale, first_ref):
    return jnp.where(first_ref[0] == 1, 1.0, env_scale)


def gram_tile(p, w1, w2, y, local, scale):
    unit = jnp.maximum(jnp.maximum(peak(w1), jnp.sqrt(peak(w2))), TINY)
    inv = 1.0 / unit
    u1 = w1 * inv
    u2 = w2 * inv * inv
    y = y * inv * inv
    local = local * inv * inv * inv * scale
    sums = [dot(p, p), dot(p, u1), dot(u1, u1), dot(u1, u2), dot(u2, u2), dot(y, local)]
    row = lax.broadcasted_iota(jnp.int32, (8, 128), 0)
    tile = jnp.broadcast_to(unit, (8, 128))
    for index, value in enumerate(sums):
        tile = jnp.where(row == index, value, tile)
    return tile


def hops_kernel(env_scale, tile_ref, sent_ref, got_ref, sent_dn_ref, got_dn_ref, first_ref, out_ref):
    tile = tile_ref[...]
    inv = 1.0 / tile[7:8, 0:1]
    size = inv * inv * inv * (2 * factor(env_scale, first_ref))
    both = (sent_ref[...] * size) * (got_ref[...] * inv * inv)
    both = both + (sent_dn_ref[...] * size) * (got_dn_ref[...] * inv * inv)
    row = lax.broadcasted_iota(jnp.int32, (8, 128), 0)
    both = jnp.sum(jnp.sum(both, axis=0, keepdims=True), axis=1, keepdims=True)
    tile = jnp.where(row == 5, tile + both, tile)
    ratio = tile[7:8, :] / lane_units()[1]
    for power in range(1, 6):
        tile = jnp.where((row >= power) & (row < 6), tile * ratio, tile)
    out_ref[...] = tile


def finish_kernel(normalise, lift, *refs):
    *tile_refs, p_ref, w1_ref, w2_ref, vector_ref, energy_ref = refs
    tile = merged([ref[...] for ref in tile_refs])
    group, unit = lane_units()
    s = [tile[j : j + 1, :] for j in range(6)]
    norm_sq = s[0] if normalise else jnp.full_like(unit, LIFT * LIFT)
    s = [value / norm_sq for value in s]
    fits = ((s[2] >= 2.0**-16) | (group == 0)) & ((s[2] < 2.0**16) | (group == 7))
    e = s[1]
    h = []
    for j in range(6):
        term = s[j]
        choose = 1
        power = jnp.ones_like(e)
        for i in range(1, j + 1):
            choose = choose * (j - i + 1) // i
            power = power * (-e)
            term = term + float(choose) * power * s[j - i]
        h.append(term)
    h[2] = jnp.maximum(h[2], 0.0)
    eps = EPS / unit / unit
    rn = jnp.sqrt(h[2] + eps)
    c = h[3] / (rn * rn) - e * (eps / (rn * rn))
    low = c / 2 - jnp.sqrt((c / 2) * (c / 2) + rn * rn)
    g = jnp.sqrt(rn * rn + low * low)
    a0 = rn / g
    a1 = low / (g * rn)
    vv1 = a0 * a0 * h[0] + 2 * a0 * a1 * h[1] + a1 * a1 * h[2]
    e2 = e * (vv1 - 1.0) + (a0 * a0 * h[1] + 2 * a0 * a1 * h[2] + a1 * a1 * h[3])
    q = (-e2 * a0, a0 - e2 * a1, a1)

    def form(offset):
        squares = sum(q[i] * q[i] * h[2 * i + offset] for i in range(3))
        cross = sum(q[i] * q[j] * h[i + j + offset] for i in range(3) for j in range(i))
        return squares + 2 * cross

    rn2 = jnp.sqrt(jnp.maximum(form(0), 0.0) + eps)
    c2 = form(1) / (rn2 * rn2) - e * (eps / (rn2 * rn2))
    gap = (e2 - c2) / 2
    low2 = (e2 + c2) / 2 - jnp.sqrt(gap * gap + rn2 * rn2)
    second = low2 - e2
    g2 = jnp.sqrt(rn2 * rn2 + second * second)
    keep = rn2 / g2
    take = second / (g2 * rn2)
    c0, c1, c2 = (keep * a0 + take * q[0], keep * a1 + take * q[1], take * q[2])
    size = lift / jnp.sqrt(norm_sq)
    d0 = (c0 - e * c1 + e * e * c2) * size
    d1 = (c1 - 2 * e * c2) * size / unit
    d2 = c2 * size / unit / unit

    def pick(value):
        return jnp.max(jnp.where(fits, value, -jnp.inf), axis=1, keepdims=True)

    d0, d1, d2 = pick(d0), pick(d1), pick(d2)
    vector_ref[...] = d0 * p_ref[...] + d1 * w1_ref[...] + d2 * w2_ref[...]
    energy_ref[0] = pick(unit * (e + low2))[0, 0]


SMEM = pl.BlockSpec(memory_space=pltpu.SMEM)
CHEAP = pl.CostEstimate(flops=1, bytes_accessed=1, transcendentals=0)
TILE = jax.ShapeDtypeStruct((8, 128), jnp.float32)


def moments_kernel(env_scale, *refs):
    y_ref, p_ref, w1_ref, w2_ref, ln, rn, lh, rh, ld, rd, first_ref = refs[:11]
    dn_ref, up_ref, tile_ref, local_ref = refs[11:]
    step = pl.program_id(0)
    parts = split(y_ref[...])
    terms = (
        pair_term(False, ln[0], rn[0], parts),
        pair_term(False, lh[0], rh[0], parts),
        pair_term(True, ld[0], rd[0], parts),
    )

    @pl.when(step == 0)
    def _():
        for ref, term in zip((dn_ref, up_ref, local_ref), terms):
            ref[...] = term

    @pl.when(step > 0)
    def _():
        for ref, term in zip((dn_ref, up_ref, local_ref), terms):
            ref[...] += term

    @pl.when(step == pl.num_programs(0) - 1)
    def _():
        tile_ref[...] = gram_tile(
            p_ref[...], w1_ref[...], w2_ref[...], y_ref[...], local_ref[...],
            factor(env_scale, first_ref),
        )


def first_moments(env_scale, first, y, p, w1, w2, envs):
    channels, width, _ = envs[0].shape
    whole = pl.BlockSpec((width, width), lambda w: (0, 0))
    env = pl.BlockSpec((1, width, width), lambda w: (w, 0, 0))
    block = jax.ShapeDtypeStruct((width, width), jnp.float32)
    return pl.pallas_call(
        functools.partial(moments_kernel, env_scale),
        grid=(channels,),
        out_shape=(block, block, TILE),
        in_specs=[whole] * 4 + [env] * 6 + [SMEM],
        out_specs=(whole, whole, pl.BlockSpec((8, 128), lambda w: (0, 0))),
        scratch_shapes=[pltpu.VMEM((width, width), jnp.float32)],
        compiler_params=pltpu.CompilerParams(vmem_limit_bytes=ROOM),
        cost_estimate=CHEAP,
        name="moments",
    )(y, p, w1, w2, *envs, first)


def add_hops(env_scale, first, tile, sent, got, sent_dn, got_dn):
    return pl.pallas_call(
        functools.partial(hops_kernel, env_scale),
        out_shape=TILE,
        in_specs=[VMEM] * 5 + [SMEM],
        out_specs=VMEM,
        cost_estimate=CHEAP,
        name="add_hops",
    )(tile, sent, got, sent_dn, got_dn, first)


def finish(normalise, lift, tiles, p, w1, w2):
    return pl.pallas_call(
        functools.partial(finish_kernel, normalise, lift),
        out_shape=(
            jax.ShapeDtypeStruct(p.shape, jnp.float32),
            jax.ShapeDtypeStruct((1,), jnp.float32),
        ),
        in_specs=[VMEM] * (len(tiles) + 3),
        out_specs=(VMEM, SMEM),
        cost_estimate=CHEAP,
        name="finish",
    )(*tiles, p, w1, w2)


def forward_pair(left_env, state_block, right_env):
    inner_term = jnp.einsum("wab,bc->wac", left_env, state_block, precision=high)
    return jnp.einsum("wac,wdc->ad", inner_term, right_env, precision=high)


def backward_pair(left_env, state_block, right_env):
    inner_term = jnp.einsum("wba,bc->wac", left_env, state_block, precision=high)
    return jnp.einsum("wac,wcd->ad", inner_term, right_env, precision=high)


def split(x):
    top = x.astype(jnp.bfloat16)
    return top, (x - top.astype(jnp.float32)).astype(jnp.bfloat16)


def product(a, b, flip=False):
    dims = (((1,), (1 if flip else 0,)), ((), ()))

    def one(x, y):
        return lax.dot_general(x, y, dims, preferred_element_type=jnp.float32)

    (a0, a1), (b0, b1) = a, b
    return one(a0, b0) + (one(a0, b1) + one(a1, b0))


def pair_term(forward, left, right, x):
    if forward:
        return product(split(product(split(left), x)), split(right), flip=True)
    return product(split(product(split(left.T), x)), split(right))


def shards(
    psi_start, kept_sizes, left_diag, left_hop, left_hop_dn, right_diag, right_hop, right_hop_dn
):
    width = psi_start.shape[-1]
    count = lax.axis_size("blk")
    sections = lax.axis_size("sect")
    stride = max(2, count // 8)
    up_pairs, dn_pairs = chain(count, stride)
    kept_count = kept_sizes[0, 0]
    row_index = lax.broadcasted_iota(jnp.int32, (width, width), 0)
    col_index = lax.broadcasted_iota(jnp.int32, (width, width), 1)
    kept_mask = (row_index < kept_count) & (col_index < kept_count)
    diag_right = right_diag[0, 0]
    hop_right = right_hop[0, 0]
    hopdn_right = right_hop_dn[0, 0]

    def base_operator(y, lefts, extra=(), tied=False):
        diag_left, hop_left, hopdn_left = lefts
        lower_dn = lax.ppermute(y, "blk", dn_pairs)
        sent_dn = backward_pair(hopdn_left, y, hopdn_right)
        if tied:
            y, sent_dn = lax.optimization_barrier((y, sent_dn))
        upper_dn = lax.ppermute(sent_dn, "blk", flipped(dn_pairs))
        lower = lax.ppermute(y, "blk", up_pairs)
        sent = backward_pair(hop_left, y, hop_right)
        upper = lax.ppermute(sent, "blk", flipped(up_pairs))
        image = forward_pair(diag_left, y, diag_right)
        image = image + forward_pair(hopdn_left, lower_dn, hopdn_right)
        image = image + forward_pair(hop_left, lower, hop_right)
        image, extra = lax.optimization_barrier((image, extra))
        return image + upper + upper_dn, extra

    def moments(env_scale, p, w1, w2, y, lefts, extra=()):
        diag_left, hop_left, hopdn_left = lefts
        envs = (hopdn_left, hopdn_right, hop_left, hop_right, diag_left, diag_right)
        got_dn = lax.ppermute(y, "blk", dn_pairs)
        sent_dn, sent, tile = first_moments(env_scale, first, y, p, w1, w2, envs)
        got = lax.ppermute(y, "blk", up_pairs)
        tile, extra = lax.optimization_barrier((tile, extra))
        return spread(add_hops(env_scale, first, tile, sent, got, sent_dn, got_dn)), extra

    lefts = (left_diag[0, 0], left_hop[0, 0], left_hop_dn[0, 0])
    to_next = [(s, s + 1) for s in range(sections - 1)]
    first_section = lax.axis_index("sect") == 0
    env_scale = float(count * width)
    env_factor = jnp.where(first_section, 1.0, env_scale)

    moved = [lax.ppermute(own, "sect", to_next) for own in lefts]

    def chosen(index):
        return jnp.where(first_section, lefts[index], moved[index])

    first = jnp.reshape(first_section.astype(jnp.int32), (1,))
    p = jnp.where(kept_mask, psi_start[0, 0], 0.0)
    w1, _ = base_operator(p, lefts)
    w1 = jnp.where(kept_mask, w1, 0.0)
    w2, hopdn_next = base_operator(w1, lefts, chosen(2))
    w2 = jnp.where(kept_mask, w2, 0.0)
    tiles, hop_next = moments(1.0, p, w1, w2, w2, lefts, chosen(1))
    tiles, diag_next = lax.optimization_barrier((tiles, chosen(0)))
    lefts_next = (diag_next, hop_next, hopdn_next)
    vector, _ = finish(True, LIFT, tiles, p, w1, w2)

    identity = (row_index == col_index).astype(jnp.float32)
    received = lax.ppermute(vector, "sect", to_next) * (1.0 / LIFT)
    frame = jnp.where(first_section, identity, received)

    def into(x):
        return jnp.einsum("ab,bc->ac", frame, x, precision=high)

    def operator(y, tied):
        image, _ = base_operator(y, lefts_next, tied=tied)
        image = jnp.einsum("ba,bc->ac", frame, image, precision=high)
        image = env_factor * image
        return jnp.where(kept_mask, image, 0.0)

    p = vector
    w1 = operator(into(p), True)
    w2 = operator(into(w1), False)
    tiles, _ = moments(env_scale, p, w1, w2, into(w2), lefts_next)
    vector, energy = finish(False, 1.0, tiles, p, w1, w2)
    return (vector[None, None], energy)


def solution(mesh):
    in_specs = (
        P("sect", "blk", None, None),
        P("sect", "blk"),
        P("sect", "blk", None, None, None),
        P("sect", "blk", None, None, None),
        P("sect", "blk", None, None, None),
        P("sect", "blk", None, None, None),
        P("sect", "blk", None, None, None),
        P("sect", "blk", None, None, None),
    )
    out_specs = (P("sect", "blk", None, None), P("sect"))
    return jax.shard_map(shards, mesh=mesh, in_specs=in_specs, out_specs=out_specs, check_vma=False)
```
